1024 devices in a mesh: replica: 16 (over x, y), owner: 64 (over z, core).
Axes of the slice: x: 4, y: 4, z: 32, core: 2. Of those that a mesh axis runs over, the one named last changes fastest.
Arguments:
- grad_parts: bfloat16 [16, 96, 512, 512], P('replica', None, 'owner'), may hold values from -1.5 to 1.5
- block_owner: int32 [96], replicated, may hold values from 0 to 63, as said below
- left_basis: float32 [128, 512, 512], P('owner'), may hold values from -0.25 to 0.25
- right_basis: float32 [128, 512, 512], P('owner'), may hold values from -0.25 to 0.25
- first_moment: bfloat16 [128, 512, 512], P('owner'), may hold values from -0.59765625 to 0.59765625
- second_moment: bfloat16 [128, 512, 512], P('owner'), may hold values from 0.0099487305 to 0.099609375
Outputs:
- direction: bfloat16 [96, 512, 512], P(None, 'owner')
- new_first: bfloat16 [128, 512, 512], P('owner')
- new_second: bfloat16 [128, 512, 512], P('owner')
The draws below stay inside these ranges and needn't reach their ends.
Inputs may be any that keep to these rules, and one draw needn't show every extreme that they name: `block_owner`: every owner is named by one or two blocks (at most 2).
All inputs are finite; a program needn't handle non-finite values.
Results may differ from the reference program's by a relative error of at most 0.024.
Values may be sent and summed in bfloat16 or wider, within the bound.
No kernel may reach another device: no remote copies, remote signals or barrier semaphores. Data moves between devices by JAX's collectives and lax.ppermute only.
A program may use at most 32 MiB of HBM per device.

```python
import math
import jax
import jax.numpy as jnp
from jax import lax

BLOCK = 512
SLOTS = 2
BLOCKS = 96
N_REPLICA = 16
N_OWNER = 64


def draw_block_owner(key, part):
    key = jax.random.fold_in(key, 11)
    key_one, key_two, key_three = jax.random.split(key, 3)
    first = jax.random.permutation(key_one, N_OWNER)
    second = jax.random.permutation(key_two, N_OWNER)[:BLOCKS - N_OWNER]
    owners = jnp.concatenate([first, second]).astype(jnp.int32)
    order = jax.random.permutation(key_three, BLOCKS)
    return owners[order].astype(jnp.int32)


def steps_of(rng, extent, shards, low, top_value):
    def one(dim, blocks):
        draws = jax.random.uniform(jax.random.fold_in(jax.random.fold_in(rng, 6), dim), (blocks,), jnp.float32, low / len(shards), top_value / len(shards))
        return jnp.repeat(jnp.exp(draws), extent[dim] // blocks).reshape((-1,) + (1,) * (len(extent) - dim - 1))

    level = one(*shards[0])
    for cut in shards[1:]:
        level = level * one(*cut)
    return level


def noise(key, shape, scale, limit, cuts=(), kind=jnp.bfloat16):
    gain = steps_of(key, shape, cuts, -0.22, 0.18) if cuts else 1.0
    drawn = jax.random.normal(key, shape, jnp.float32) * scale * gain
    return jnp.minimum(jnp.maximum(drawn, -limit), limit).astype(kind)


def setup_inputs(seed: int = 0) -> dict:
    arg_keys = jax.random.split(jax.random.key(seed), 7)
    return {
        "grad_parts": noise(arg_keys[0], (N_REPLICA, BLOCKS, BLOCK, BLOCK), 0.25, 1.5, ((0, 16), (2, 64))),
        "block_owner": draw_block_owner(jax.random.fold_in(arg_keys[6], 71), 0),
        "left_basis": noise(arg_keys[2], (N_OWNER * SLOTS, BLOCK, BLOCK), BLOCK ** -0.5, 0.25, ((0, 64),), jnp.float32),
        "right_basis": noise(arg_keys[3], (N_OWNER * SLOTS, BLOCK, BLOCK), BLOCK ** -0.5, 0.25, ((0, 64),), jnp.float32),
        "first_moment": noise(arg_keys[4], (N_OWNER * SLOTS, BLOCK, BLOCK), 0.1, 0.59765625, ((0, 64),)),
        "second_moment": jnp.clip(jnp.exp(math.log(0.099609375) - 2.3038113 * jax.random.uniform(arg_keys[5], (N_OWNER * SLOTS, BLOCK, BLOCK), jnp.float32) ** steps_of(arg_keys[5], (N_OWNER * SLOTS, BLOCK, BLOCK), ((0, 64),), -0.2, 0.2)), 0.0099487305, 0.099609375).astype(jnp.bfloat16),
    }


beta_first = 0.9
beta_second = 0.95
bias_first = 1.0 - 0.9 ** 20
bias_second = 1.0 - 0.95 ** 20
epsilon = 1e-08

def one_slot(items):
    left, right, grad_block, first_old, second_old = items
    rotated = jnp.dot(left.T, grad_block.astype(jnp.float32), precision=lax.Precision.HIGHEST)
    rotated = jnp.dot(rotated, right, precision=lax.Precision.HIGHEST)
    first = beta_first * first_old.astype(jnp.float32) + (1.0 - beta_first) * rotated
    second = beta_second * second_old.astype(jnp.float32) + (1.0 - beta_second) * rotated * rotated
    update = (first / bias_first / (jnp.sqrt(second / bias_second) + epsilon)).astype(jnp.bfloat16)
    left_half = jnp.dot(left.astype(jnp.bfloat16), update, preferred_element_type=jnp.float32).astype(jnp.bfloat16)
    slot_dir = jnp.dot(left_half, right.astype(jnp.bfloat16).T, preferred_element_type=jnp.float32).astype(jnp.bfloat16)
    return (slot_dir, first.astype(jnp.bfloat16), second.astype(jnp.bfloat16))

def reference(grad_parts, block_owner, left_basis, right_basis, first_moment, second_moment):
    gradient = lax.optimization_barrier(jnp.sum(grad_parts.astype(jnp.float32), axis=0)).astype(jnp.bfloat16)
    index = jnp.arange(BLOCKS, dtype=jnp.int32)
    same = block_owner[:, None] == block_owner[None, :]
    earlier = index[None, :] < index[:, None]
    level = lax.optimization_barrier(jnp.sum((same & earlier).astype(jnp.int32), axis=1)).astype(jnp.int32)
    slot = (block_owner * SLOTS + level).astype(jnp.int32)
    slot_grad = jnp.zeros((N_OWNER * SLOTS, BLOCK, BLOCK), jnp.bfloat16).at[slot].set(gradient)
    slot_dir, new_first, new_second = lax.map(one_slot, (left_basis, right_basis, slot_grad, first_moment, second_moment))
    direction = slot_dir[slot]
    return (direction, new_first, new_second)
```

```python
import functools

import jax
import jax.numpy as jnp
from jax import lax
from jax.experimental import pallas as pl
from jax.experimental.pallas import tpu as pltpu
from jax.sharding import PartitionSpec as P

beta_first = 0.9
beta_second = 0.95
bias_first = 1.0 - 0.9**20
bias_second = 1.0 - 0.95**20
epsilon = 1e-08

PAIRS = 4
TILES = 4
PIECES = PAIRS * TILES
LANES = 128
GROUP = 16

f32 = jnp.float32
bf16 = jnp.bfloat16


def dot(a, b):
    return jnp.dot(a, b, preferred_element_type=f32)


def permutation(dtype):
    out = lax.broadcasted_iota(jnp.int32, (8 * GROUP, 8 * GROUP), 0)
    src = lax.broadcasted_iota(jnp.int32, (8 * GROUP, 8 * GROUP), 1)
    pair = out >> 5
    block = (out & 31) >> 1
    return (src == block * 8 + pair * 2 + (out & 1)).astype(dtype)


def inverse_permutation(dtype):
    out = lax.broadcasted_iota(jnp.int32, (8 * GROUP, 8 * GROUP), 0)
    src = lax.broadcasted_iota(jnp.int32, (8 * GROUP, 8 * GROUP), 1)
    pair = src >> 5
    block = (src & 31) >> 1
    return (out == block * 8 + pair * 2 + (src & 1)).astype(dtype)


def cut_kernel(strips, pieces):
    perm = permutation(bf16)
    for g in range(strips.shape[0] // (8 * GROUP)):
        moved = dot(perm, strips[g * 128 : (g + 1) * 128, :]).astype(bf16)
        for pair in range(PAIRS):
            for tile in range(TILES):
                pieces[pair * TILES + tile, g * 32 : (g + 1) * 32, :] = moved[
                    pair * 32 : (pair + 1) * 32, tile * LANES : (tile + 1) * LANES
                ]


def join_kernel(pieces, strips):
    perm = inverse_permutation(bf16)
    for g in range(strips.shape[0] // (8 * GROUP)):
        rows = [
            jnp.concatenate(
                [pieces[pair * TILES + tile, g * 32 : (g + 1) * 32, :] for tile in range(TILES)],
                axis=1,
            )
            for pair in range(PAIRS)
        ]
        strips[g * 128 : (g + 1) * 128, :] = dot(perm, jnp.concatenate(rows, axis=0)).astype(bf16)


def prep_kernel(owner_col, owner_row, left, right, place, pick, left_p, left_t, right_b, right_t):
    perm = permutation(bf16)
    count2 = owner_row.shape[1]
    col = lax.broadcasted_iota(jnp.int32, (count2, count2), 0) >> 1
    row = lax.broadcasted_iota(jnp.int32, (count2, count2), 1) >> 1
    same = owner_col[...] == owner_row[...]
    level_row = jnp.sum((same & (col < row)).astype(f32), axis=0, keepdims=True) * 0.5
    level_col = jnp.sum((same & (row < col)).astype(f32), axis=1, keepdims=True) * 0.5
    for level in range(2):
        out = lax.broadcasted_iota(jnp.int32, (128, count2), 0)
        src = lax.broadcasted_iota(jnp.int32, (128, count2), 1)
        hit = (owner_row[...] == (out >> 1)) & (level_row == level) & ((out & 1) == (src & 1))
        place[level, :, :] = hit.astype(bf16)
        out = lax.broadcasted_iota(jnp.int32, (count2, 128), 0)
        src = lax.broadcasted_iota(jnp.int32, (count2, 128), 1)
        hit = (owner_col[...] == (src >> 1)) & (level_col == level) & ((out & 1) == (src & 1))
        pick[level, :, :] = hit.astype(bf16)
        parts = [
            dot(perm, left[level, g * 128 : (g + 1) * 128, :].astype(bf16)) for g in range(PAIRS)
        ]
        for pair in range(PAIRS):
            here = jnp.concatenate([part[pair * 32 : (pair + 1) * 32] for part in parts], axis=0)
            left_p[level, pair * 128 : (pair + 1) * 128, :] = here.astype(bf16)
            left_t[level, :, pair * 128 : (pair + 1) * 128] = here.T.astype(bf16)
        right_b[level, :, :] = right[level, :, :].astype(bf16)
        right_t[level, :, :] = right[level, :, :].T.astype(bf16)


def place_kernel(pieces, place, placed):
    total = pieces[0].astype(f32)
    for k in range(1, PIECES):
        total = total + pieces[k].astype(f32)
    total = total.astype(bf16)
    for level in range(2):
        placed[:, level * LANES : (level + 1) * LANES] = dot(place[level], total).astype(bf16)


def step_kernel(
    where, gathered, left_p, left_t, right_b, right_t, first_old, second_old, piece, first_new, second_new
):
    for level in range(2):
        lanes = slice(level * LANES, (level + 1) * LANES)
        grad = jnp.concatenate(
            [
                jnp.concatenate(
                    [gathered[pair * TILES + tile, :, lanes] for tile in range(TILES)], axis=1
                )
                for pair in range(PAIRS)
            ],
            axis=0,
        )
        half = dot(left_t[level], grad).astype(bf16)
        rotated = dot(half, right_b[level])
        first = beta_first * first_old[level].astype(f32) + (1.0 - beta_first) * rotated
        second = (
            beta_second * second_old[level].astype(f32) + (1.0 - beta_second) * rotated * rotated
        )
        first_new[level, :, :] = first.astype(bf16)
        second_new[level, :, :] = second.astype(bf16)
        update = ((first / bias_first) / (jnp.sqrt(second / bias_second) + epsilon)).astype(bf16)
        mine = left_p[level, pl.ds(pl.multiple_of(where[0] * 128, 128), 128), :]
        left_half = dot(mine, update).astype(bf16)
        turned = right_t[level, :, pl.ds(pl.multiple_of(where[1] * LANES, LANES), LANES)]
        piece[:, lanes] = dot(left_half, turned).astype(bf16)


def pick_kernel(returned, pick, copies):
    mine = (dot(pick[0], returned[:, :LANES]) + dot(pick[1], returned[:, LANES:])).astype(bf16)
    for k in range(PIECES):
        copies[k, :, :] = mine


VMEM = pl.BlockSpec(memory_space=pltpu.VMEM)
SMEM = pl.BlockSpec(memory_space=pltpu.SMEM)


def shape(dims, dtype):
    return jax.ShapeDtypeStruct(dims, dtype)


def call(kernel, out, inputs, specs=None, scratch=(), limit=32, cost=None):
    single = not isinstance(out, (list, tuple))
    return pl.pallas_call(
        kernel,
        out_shape=out,
        in_specs=specs or [VMEM] * len(inputs),
        out_specs=VMEM if single else [VMEM] * len(out),
        scratch_shapes=scratch,
        cost_estimate=cost,
        compiler_params=pltpu.CompilerParams(vmem_limit_bytes=limit * 2**20),
    )(*inputs)


def local(grad_parts, block_owner, left_basis, right_basis, first_moment, second_moment):
    count, rows, width = grad_parts.shape[1:]
    replica = lax.axis_index("replica")
    owner2 = jnp.repeat(block_owner, 2)
    strips = grad_parts.reshape(count * rows, width)
    pieces = call(cut_kernel, shape((PIECES, count * 2, LANES), bf16), (strips,))
    parts = lax.all_to_all(pieces, "replica", 0, 0)
    wide = shape((2, width, width), bf16)
    place, pick, left_p, left_t, right_b, right_t = call(
        prep_kernel,
        [shape((2, 128, count * 2), bf16), shape((2, count * 2, 128), bf16), wide, wide, wide, wide],
        (owner2[:, None], owner2[None, :], left_basis, right_basis),
        cost=pl.CostEstimate(flops=4 * 10**9, bytes_accessed=8 * 2**20, transcendentals=0),
    )
    placed = call(place_kernel, shape((128, 2 * LANES), bf16), (parts, place))
    moved = lax.all_to_all(placed.reshape(64, 2, 2 * LANES), "owner", 0, 0).reshape(128, 2 * LANES)
    gathered = lax.all_to_all(
        jnp.broadcast_to(moved[None], (PIECES, 128, 2 * LANES)), "replica", 0, 0
    )
    where = jnp.stack([replica // TILES, replica % TILES]).astype(jnp.int32)
    piece, first, second = call(
        step_kernel,
        [shape((128, 2 * LANES), bf16), wide, wide],
        (where, gathered, left_p, left_t, right_b, right_t, first_moment, second_moment),
        specs=[SMEM] + [VMEM] * 7,
    )
    returned = lax.all_to_all(piece.reshape(64, 2, 2 * LANES), "owner", 0, 0)
    copies = call(
        pick_kernel,
        shape((PIECES, count * 2, LANES), bf16),
        (returned.reshape(128, 2 * LANES), pick),
    )
    joined = lax.all_to_all(copies, "replica", 0, 0)
    direction = call(join_kernel, shape((count * rows, width), bf16), (joined,))
    return direction.reshape(count, rows, width), first, second


def solution(mesh):
    return jax.shard_map(
        local,
        mesh=mesh,
        in_specs=(
            P("replica", None, "owner", None),
            P(),
            P("owner", None, None),
            P("owner", None, None),
            P("owner", None, None),
            P("owner", None, None),
        ),
        out_specs=(P(None, "owner", None), P("owner", None, None), P("owner", None, None)),
        check_vma=False,
    )
```

```python
import functools

import jax
import jax.numpy as jnp
from jax import lax
from jax.experimental import pallas as pl
from jax.experimental.pallas import tpu as pltpu
from jax.sharding import PartitionSpec as P

beta_first = 0.9
beta_second = 0.95
bias_first = 1.0 - 0.9**20
bias_second = 1.0 - 0.95**20
epsilon = 1e-08

PAIRS = 4
TILES = 4
PIECES = PAIRS * TILES
LANES = 128
GROUP = 16

f32 = jnp.float32
bf16 = jnp.bfloat16


def dot(a, b):
    return jnp.dot(a, b, preferred_element_type=f32)


def permutation(dtype):
    out = lax.broadcasted_iota(jnp.int32, (8 * GROUP, 8 * GROUP), 0)
    src = lax.broadcasted_iota(jnp.int32, (8 * GROUP, 8 * GROUP), 1)
    pair = out >> 5
    block = (out & 31) >> 1
    return (src == block * 8 + pair * 2 + (out & 1)).astype(dtype)


def inverse_permutation(dtype):
    out = lax.broadcasted_iota(jnp.int32, (8 * GROUP, 8 * GROUP), 0)
    src = lax.broadcasted_iota(jnp.int32, (8 * GROUP, 8 * GROUP), 1)
    pair = src >> 5
    block = (src & 31) >> 1
    return (out == block * 8 + pair * 2 + (src & 1)).astype(dtype)


def cut_kernel(owner, strips, pieces, slots):
    count = owner.shape[1]
    across = jnp.broadcast_to(owner[...], (count, count)).astype(f32)
    earlier = lax.broadcasted_iota(jnp.int32, (count, count), 0) < lax.broadcasted_iota(
        jnp.int32, (count, count), 1
    )
    level = jnp.sum(((across == across.T) & earlier).astype(f32), axis=0, keepdims=True)
    slot = 2.0 * owner[...].astype(f32) + level
    double = lax.broadcasted_iota(jnp.int32, (count, 2 * count), 0) == (
        lax.broadcasted_iota(jnp.int32, (count, 2 * count), 1) >> 1
    )
    slots[...] = dot(slot.astype(bf16), double.astype(bf16))
    perm = permutation(bf16)
    for g in range(strips.shape[0] // (8 * GROUP)):
        moved = dot(perm, strips[g * 128 : (g + 1) * 128, :]).astype(bf16)
        for pair in range(PAIRS):
            for tile in range(TILES):
                pieces[pair * TILES + tile, g * 32 : (g + 1) * 32, :] = moved[
                    pair * 32 : (pair + 1) * 32, tile * LANES : (tile + 1) * LANES
                ]


def join_kernel(pieces, strips):
    perm = inverse_permutation(bf16)
    for g in range(strips.shape[0] // (8 * GROUP)):
        rows = [
            jnp.concatenate(
                [pieces[pair * TILES + tile, g * 32 : (g + 1) * 32, :] for tile in range(TILES)],
                axis=1,
            )
            for pair in range(PAIRS)
        ]
        strips[g * 128 : (g + 1) * 128, :] = dot(perm, jnp.concatenate(rows, axis=0)).astype(bf16)


def onehot(slots, level):
    dims = (128, slots.shape[1])
    out = lax.broadcasted_iota(jnp.int32, dims, 0)
    src = lax.broadcasted_iota(jnp.int32, dims, 1)
    here = slots[...] == (2 * (out >> 1) + level).astype(f32)
    return (here & ((out & 1) == (src & 1))).astype(bf16)


def place_kernel(pieces, slots, placed):
    total = pieces[0].astype(f32)
    for k in range(1, PIECES):
        total = total + pieces[k].astype(f32)
    total = total.astype(bf16)
    for level in range(2):
        lanes = slice(level * LANES, (level + 1) * LANES)
        placed[:, lanes] = dot(onehot(slots, level), total).astype(bf16)


def spread_kernel(moved, copies):
    for k in range(PIECES):
        copies[k, :, :] = moved[...]


def step_kernel(
    gathered, left, right, first_old, second_old, piece, first_new, second_new,
    second_held, first_buf, second_buf, rows, cols, sems, load_sem,
):
    replica = lax.axis_index("replica")
    pair, tile = lax.shift_right_logical(replica, 2), replica & 3
    perm = permutation(bf16)
    load = pltpu.make_async_copy(second_old, second_held, load_sem)
    load.start()
    copies = []
    for level in range(2):
        lanes = slice(level * LANES, (level + 1) * LANES)
        parts = [
            dot(perm, left[level, g * 128 : (g + 1) * 128, :].astype(bf16)) for g in range(PAIRS)
        ]
        turned = []
        for k in range(PAIRS):
            here = jnp.concatenate([part[k * 32 : (k + 1) * 32] for part in parts], axis=0)
            rows[level, k * 128 : (k + 1) * 128, :] = here.astype(bf16)
            turned.append(here.T.astype(bf16))
        left_t = jnp.concatenate(turned, axis=1)
        right_b = right[level].astype(bf16)
        cols[level, :, :] = right[level].T.astype(bf16)
        grad = jnp.concatenate(
            [
                jnp.concatenate(
                    [gathered[pair * TILES + tile, :, lanes] for tile in range(TILES)], axis=1
                )
                for pair in range(PAIRS)
            ],
            axis=0,
        )
        half = dot(left_t, grad).astype(bf16)
        rotated = dot(half, right_b)
        if level == 0:
            load.wait()
        first = beta_first * first_old[level].astype(f32) + (1.0 - beta_first) * rotated
        second = (
            beta_second * second_held[level].astype(f32) + (1.0 - beta_second) * rotated * rotated
        )
        first_buf[level, :, :] = first.astype(bf16)
        second_buf[level, :, :] = second.astype(bf16)
        for k, (buf, new) in enumerate([(first_buf, first_new), (second_buf, second_new)]):
            copy = pltpu.make_async_copy(buf.at[level], new.at[level], sems.at[level, k])
            copy.start()
            copies.append(copy)
        update = ((first / bias_first) / (jnp.sqrt(second / bias_second) + epsilon)).astype(bf16)
        mine = rows[level, pl.ds(pl.multiple_of(pair * 128, 128), 128), :]
        left_half = dot(mine, update).astype(bf16)
        back = cols[level, :, pl.ds(pl.multiple_of(tile * LANES, LANES), LANES)]
        piece[:, lanes] = dot(left_half, back).astype(bf16)
    for copy in copies:
        copy.wait()


def pick_kernel(returned, slots, copies):
    mine = sum(
        lax.dot_general(
            onehot(slots, level),
            returned[:, level * LANES : (level + 1) * LANES],
            (((0,), (0,)), ((), ())),
            preferred_element_type=f32,
        )
        for level in range(2)
    ).astype(bf16)
    for k in range(PIECES):
        copies[k, :, :] = mine


VMEM = pl.BlockSpec(memory_space=pltpu.VMEM)
ANY = pl.BlockSpec(memory_space=pl.ANY)


def shape(dims, dtype):
    return jax.ShapeDtypeStruct(dims, dtype)


def call(kernel, out, inputs, specs=None, outs=None, scratch=(), limit=8, cost=None):
    single = not isinstance(out, (list, tuple))
    return pl.pallas_call(
        kernel,
        out_shape=out,
        in_specs=specs or [VMEM] * len(inputs),
        out_specs=outs or (VMEM if single else [VMEM] * len(out)),
        scratch_shapes=scratch,
        cost_estimate=cost,
        compiler_params=pltpu.CompilerParams(vmem_limit_bytes=limit * 2**20),
    )(*inputs)


def local(grad_parts, block_owner, left_basis, right_basis, first_moment, second_moment):
    count, rows, width = grad_parts.shape[1:]
    strips = grad_parts.reshape(count * rows, width)
    slot_row = shape((1, 2 * count), f32)
    pieces, slots = call(
        cut_kernel,
        [shape((PIECES, count * 2, LANES), bf16), slot_row],
        (block_owner[None, :], strips),
    )
    parts = lax.all_to_all(pieces, "replica", 0, 0)
    wide = shape((2, width, width), bf16)
    placed = call(place_kernel, shape((128, 2 * LANES), bf16), (parts, slots))
    moved = lax.all_to_all(placed.reshape(64, 2, 2 * LANES), "owner", 0, 0).reshape(128, 2 * LANES)
    copies = call(spread_kernel, shape((PIECES, 128, 2 * LANES), bf16), (moved,))
    gathered = lax.all_to_all(copies, "replica", 0, 0)
    piece, first, second = call(
        step_kernel,
        [shape((128, 2 * LANES), bf16), wide, wide],
        (gathered, left_basis, right_basis, first_moment, second_moment),
        specs=[VMEM] * 4 + [ANY],
        outs=[VMEM, ANY, ANY],
        scratch=[pltpu.VMEM((2, width, width), bf16)] * 5
        + [
            pltpu.SemaphoreType.DMA((2, 2)),
            pltpu.SemaphoreType.DMA,
        ],
        limit=16,
    )
    returned = lax.all_to_all(piece.reshape(64, 2, 2 * LANES), "owner", 0, 0)
    copies = call(
        pick_kernel,
        shape((PIECES, count * 2, LANES), bf16),
        (returned.reshape(128, 2 * LANES), slots),
    )
    joined = lax.all_to_all(copies, "replica", 0, 0)
    direction = call(join_kernel, shape((count * rows, width), bf16), (joined,))
    return direction.reshape(count, rows, width), first, second


def solution(mesh):
    return jax.shard_map(
        local,
        mesh=mesh,
        in_specs=(
            P("replica", None, "owner", None),
            P(),
            P("owner", None, None),
            P("owner", None, None),
            P("owner", None, None),
            P("owner", None, None),
        ),
        out_specs=(P(None, "owner", None), P("owner", None, None), P("owner", None, None)),
        check_vma=False,
    )
```

```python
import functools

import jax
import jax.numpy as jnp
from jax import lax
from jax.experimental import pallas as pl
from jax.experimental.pallas import tpu as pltpu
from jax.sharding import PartitionSpec as P

beta_first = 0.9
beta_second = 0.95
bias_first = 1.0 - 0.9**20
bias_second = 1.0 - 0.95**20
epsilon = 1e-08

PAIRS = 4
TILES = 4
PIECES = PAIRS * TILES
LANES = 128
GROUP = 16

f32 = jnp.float32
bf16 = jnp.bfloat16


def dot(a, b):
    return jnp.dot(a, b, preferred_element_type=f32)


def permutation(dtype):
    out = lax.broadcasted_iota(jnp.int32, (8 * GROUP, 8 * GROUP), 0)
    src = lax.broadcasted_iota(jnp.int32, (8 * GROUP, 8 * GROUP), 1)
    pair = out >> 5
    block = (out & 31) >> 1
    return (src == block * 8 + pair * 2 + (out & 1)).astype(dtype)


def inverse_permutation(dtype):
    out = lax.broadcasted_iota(jnp.int32, (8 * GROUP, 8 * GROUP), 0)
    src = lax.broadcasted_iota(jnp.int32, (8 * GROUP, 8 * GROUP), 1)
    pair = src >> 5
    block = (src & 31) >> 1
    return (out == block * 8 + pair * 2 + (src & 1)).astype(dtype)


def cut_kernel(strips_hbm, pieces, strips, sems):
    groups = strips.shape[0] // (8 * GROUP)
    loads = []
    for g in range(groups):
        part = pl.ds(g * 128, 128)
        loads.append(pltpu.make_async_copy(strips_hbm.at[part], strips.at[part], sems.at[g]))
        loads[-1].start()
    perm = permutation(bf16)
    for g in range(groups):
        loads[g].wait()
        moved = dot(perm, strips[g * 128 : (g + 1) * 128, :]).astype(bf16)
        for pair in range(PAIRS):
            for tile in range(TILES):
                pieces[pair * TILES + tile, g * 32 : (g + 1) * 32, :] = moved[
                    pair * 32 : (pair + 1) * 32, tile * LANES : (tile + 1) * LANES
                ]


def join_kernel(pieces, strips_hbm, strips, sems):
    perm = inverse_permutation(bf16)
    stores = []
    for g in range(strips.shape[0] // (8 * GROUP)):
        rows = [
            jnp.concatenate(
                [pieces[pair * TILES + tile, g * 32 : (g + 1) * 32, :] for tile in range(TILES)],
                axis=1,
            )
            for pair in range(PAIRS)
        ]
        part = pl.ds(g * 128, 128)
        strips[g * 128 : (g + 1) * 128, :] = dot(perm, jnp.concatenate(rows, axis=0)).astype(bf16)
        stores.append(pltpu.make_async_copy(strips.at[part], strips_hbm.at[part], sems.at[g]))
        stores[-1].start()
    for store in stores:
        store.wait()


def onehot(slots, level):
    dims = (128, slots.shape[1])
    out = lax.broadcasted_iota(jnp.int32, dims, 0)
    src = lax.broadcasted_iota(jnp.int32, dims, 1)
    here = slots[...] == (2 * (out >> 1) + level).astype(f32)
    return (here & ((out & 1) == (src & 1))).astype(bf16)


def prep_kernel(
    owner, left, right, slots, mine, left_t, right_b, turned, rows, cols, left_buf, right_buf, sems
):
    count = owner.shape[1]
    across = jnp.broadcast_to(owner[...], (count, count)).astype(f32)
    earlier = lax.broadcasted_iota(jnp.int32, (count, count), 0) < lax.broadcasted_iota(
        jnp.int32, (count, count), 1
    )
    level = jnp.sum(((across == across.T) & earlier).astype(f32), axis=0, keepdims=True)
    slot = 2.0 * owner[...].astype(f32) + level
    double = lax.broadcasted_iota(jnp.int32, (count, 2 * count), 0) == (
        lax.broadcasted_iota(jnp.int32, (count, 2 * count), 1) >> 1
    )
    slots[...] = dot(slot.astype(bf16), double.astype(bf16))
    replica = lax.axis_index("replica")
    pair, tile = lax.shift_right_logical(replica, 2), replica & 3
    perm = permutation(bf16)
    copies = []
    for level in range(2):
        parts = [
            dot(perm, left[level, g * 128 : (g + 1) * 128, :].astype(bf16)) for g in range(PAIRS)
        ]
        for k in range(PAIRS):
            here = jnp.concatenate([part[k * 32 : (k + 1) * 32] for part in parts], axis=0)
            rows[level, k * 128 : (k + 1) * 128, :] = here.astype(bf16)
            left_buf[level, :, k * 128 : (k + 1) * 128] = here.T.astype(bf16)
        right_buf[level, :, :] = right[level, :, :].astype(bf16)
        cols[level, :, :] = right[level, :, :].T.astype(bf16)
        part = pl.ds(pl.multiple_of(pair * 128, 128), 128)
        lanes = pl.ds(pl.multiple_of(tile * LANES, LANES), LANES)
        for k, (src, dst) in enumerate(
            [
                (left_buf.at[level], left_t.at[level]),
                (right_buf.at[level], right_b.at[level]),
                (rows.at[level, part], mine.at[level]),
                (cols.at[level, :, lanes], turned.at[level]),
            ]
        ):
            copies.append(pltpu.make_async_copy(src, dst, sems.at[level, k]))
            copies[-1].start()
    for copy in copies:
        copy.wait()


def place_kernel(pieces, slots, placed):
    total = pieces[0].astype(f32)
    for k in range(1, PIECES):
        total = total + pieces[k].astype(f32)
    total = total.astype(bf16)
    for level in range(2):
        lanes = slice(level * LANES, (level + 1) * LANES)
        placed[:, lanes] = dot(onehot(slots, level), total).astype(bf16)


def spread_kernel(moved, copies):
    for k in range(PIECES):
        for level in range(2):
            copies[k, level * 128 : (level + 1) * 128, :] = moved[
                :, level * LANES : (level + 1) * LANES
            ]


def step_kernel(
    gathered, mine, left_t, right_b, turned, first_old, second_old, piece, first_new, second_new,
    first_held, second_held, first_buf, second_buf, sems, load_sems,
):
    loads = []
    for level in range(2):
        for k, (old, held) in enumerate([(first_old, first_held), (second_old, second_held)]):
            load = pltpu.make_async_copy(old.at[level], held.at[level], load_sems.at[level, k])
            load.start()
            loads.append(load)
    copies = []
    for level in range(2):
        grad = jnp.concatenate(
            [
                jnp.concatenate(
                    [
                        gathered[pair * TILES + tile, level * 128 : (level + 1) * 128, :]
                        for tile in range(TILES)
                    ],
                    axis=1,
                )
                for pair in range(PAIRS)
            ],
            axis=0,
        )
        half = dot(left_t[level], grad).astype(bf16)
        rotated = dot(half, right_b[level])
        loads[2 * level].wait()
        loads[2 * level + 1].wait()
        first = beta_first * first_held[level].astype(f32) + (1.0 - beta_first) * rotated
        second = beta_second * second_held[level].astype(f32) + (
            (1.0 - beta_second) * rotated
        ) * rotated
        first_buf[level, :, :] = first.astype(bf16)
        second_buf[level, :, :] = second.astype(bf16)
        for k, (buf, new) in enumerate([(first_buf, first_new), (second_buf, second_new)]):
            copy = pltpu.make_async_copy(buf.at[level], new.at[level], sems.at[level, k])
            copy.start()
            copies.append(copy)
        scaled = second * (1.0 / bias_second)
        update = (first * (1.0 / bias_first)) / (scaled * lax.rsqrt(scaled) + epsilon)
        left_half = dot(mine[level], update.astype(bf16)).astype(bf16)
        lanes = slice(level * LANES, (level + 1) * LANES)
        piece[:, lanes] = dot(left_half, turned[level]).astype(bf16)
    for copy in copies:
        copy.wait()


def pick_kernel(returned, slots, copies):
    mine = sum(
        lax.dot_general(
            onehot(slots, level),
            returned[:, level * LANES : (level + 1) * LANES],
            (((0,), (0,)), ((), ())),
            preferred_element_type=f32,
        )
        for level in range(2)
    ).astype(bf16)
    for k in range(PIECES):
        copies[k, :, :] = mine


VMEM = pl.BlockSpec(memory_space=pltpu.VMEM)
HBM = pl.BlockSpec(memory_space=pltpu.HBM)


def shape(dims, dtype):
    return jax.ShapeDtypeStruct(dims, dtype)


def in_hbm(array):
    return pltpu.with_memory_space_constraint(array, pltpu.HBM)


def call(kernel, out, inputs, specs=None, outs=None, scratch=(), limit=8, cost=None):
    single = not isinstance(out, (list, tuple))
    return pl.pallas_call(
        kernel,
        out_shape=out,
        in_specs=specs or [VMEM] * len(inputs),
        out_specs=outs or (VMEM if single else [VMEM] * len(out)),
        scratch_shapes=scratch,
        cost_estimate=cost,
        compiler_params=pltpu.CompilerParams(vmem_limit_bytes=limit * 2**20),
    )(*inputs)


def local(grad_parts, block_owner, left_basis, right_basis, first_moment, second_moment):
    count, rows, width = grad_parts.shape[1:]
    strips = grad_parts.reshape(count * rows, width)
    slot_row = shape((1, 2 * count), f32)
    groups = count // GROUP
    pieces = call(
        cut_kernel,
        shape((PIECES, count * 2, LANES), bf16),
        (in_hbm(strips),),
        specs=[HBM],
        scratch=[
            pltpu.VMEM((count * rows, width), bf16),
            pltpu.SemaphoreType.DMA((groups,)),
        ],
    )
    parts = lax.all_to_all(pieces, "replica", 0, 0)
    wide_hbm = pltpu.HBM((2, width, width), bf16)
    held = pltpu.VMEM((2, width, width), bf16)
    slots, mine, left_t, right_b, turned = call(
        prep_kernel,
        [
            slot_row,
            pltpu.HBM((2, 128, width), bf16),
            wide_hbm,
            wide_hbm,
            pltpu.HBM((2, width, LANES), bf16),
        ],
        (block_owner[None, :], left_basis, right_basis),
        outs=[VMEM] + [HBM] * 4,
        scratch=[held] * 4 + [pltpu.SemaphoreType.DMA((2, 4))],
        limit=16,
        cost=pl.CostEstimate(flops=4 * 10**9, bytes_accessed=8 * 2**20, transcendentals=0),
    )
    placed = call(place_kernel, shape((128, 2 * LANES), bf16), (parts, slots))
    moved = lax.all_to_all(placed.reshape(64, 2, 2 * LANES), "owner", 0, 0).reshape(128, 2 * LANES)
    copies = call(spread_kernel, shape((PIECES, 2 * 128, LANES), bf16), (moved,))
    gathered = lax.all_to_all(copies, "replica", 0, 0)
    piece, first, second = call(
        step_kernel,
        [shape((128, 2 * LANES), bf16), wide_hbm, wide_hbm],
        (gathered, mine, left_t, right_b, turned, in_hbm(first_moment), in_hbm(second_moment)),
        specs=[VMEM] * 5 + [HBM] * 2,
        outs=[VMEM, HBM, HBM],
        scratch=[held] * 4 + [pltpu.SemaphoreType.DMA((2, 2))] * 2,
        limit=16,
    )
    returned = lax.all_to_all(piece.reshape(64, 2, 2 * LANES), "owner", 0, 0)
    copies = call(
        pick_kernel,
        shape((PIECES, count * 2, LANES), bf16),
        (returned.reshape(128, 2 * LANES), slots),
    )
    joined = lax.all_to_all(copies, "replica", 0, 0)
    direction = call(
        join_kernel,
        pltpu.HBM((count * rows, width), bf16),
        (joined,),
        outs=HBM,
        scratch=[
            pltpu.VMEM((count * rows, width), bf16),
            pltpu.SemaphoreType.DMA((groups,)),
        ],
    )
    return direction.reshape(count, rows, width), first, second


def solution(mesh):
    return jax.shard_map(
        local,
        mesh=mesh,
        in_specs=(
            P("replica", None, "owner", None),
            P(),
            P("owner", None, None),
            P("owner", None, None),
            P("owner", None, None),
            P("owner", None, None),
        ),
        out_specs=(P(None, "owner", None), P("owner", None, None), P("owner", None, None)),
        check_vma=False,
    )
```

```python
import functools

import jax
import jax.numpy as jnp
from jax import lax
from jax.experimental import pallas as pl
from jax.experimental.pallas import tpu as pltpu
from jax.sharding import PartitionSpec as P

beta_first = 0.9
beta_second = 0.95
bias_first = 1.0 - 0.9**20
bias_second = 1.0 - 0.95**20
epsilon = 1e-08

PAIRS = 4
TILES = 4
PIECES = PAIRS * TILES
LANES = 128
GROUP = 16

f32 = jnp.float32
bf16 = jnp.bfloat16


def dot(a, b):
    return jnp.dot(a, b, preferred_element_type=f32)


def permutation(dtype):
    out = lax.broadcasted_iota(jnp.int32, (8 * GROUP, 8 * GROUP), 0)
    src = lax.broadcasted_iota(jnp.int32, (8 * GROUP, 8 * GROUP), 1)
    pair = out >> 5
    block = (out & 31) >> 1
    return (src == block * 8 + pair * 2 + (out & 1)).astype(dtype)


def inverse_permutation(dtype):
    out = lax.broadcasted_iota(jnp.int32, (8 * GROUP, 8 * GROUP), 0)
    src = lax.broadcasted_iota(jnp.int32, (8 * GROUP, 8 * GROUP), 1)
    pair = src >> 5
    block = (src & 31) >> 1
    return (out == block * 8 + pair * 2 + (src & 1)).astype(dtype)


def cut_kernel(owner_hbm, strips_hbm, pieces, slots, owner, strips, sems):
    take = pltpu.make_async_copy(owner_hbm, owner, sems.at[0])
    take.start()
    load = pltpu.make_async_copy(strips_hbm, strips, sems.at[1])
    load.start()
    take.wait()
    count = owner.shape[1]
    across = jnp.broadcast_to(owner[...], (count, count)).astype(f32)
    earlier = lax.broadcasted_iota(jnp.int32, (count, count), 0) < lax.broadcasted_iota(
        jnp.int32, (count, count), 1
    )
    level = jnp.sum(((across == across.T) & earlier).astype(f32), axis=0, keepdims=True)
    slot = 2.0 * owner[...].astype(f32) + level
    double = lax.broadcasted_iota(jnp.int32, (count, 2 * count), 0) == (
        lax.broadcasted_iota(jnp.int32, (count, 2 * count), 1) >> 1
    )
    slots[...] = dot(slot.astype(bf16), double.astype(bf16))
    perm = permutation(bf16)
    load.wait()
    for g in range(strips.shape[0] // (8 * GROUP)):
        moved = dot(perm, strips[g * 128 : (g + 1) * 128, :]).astype(bf16)
        for pair in range(PAIRS):
            for tile in range(TILES):
                pieces[pair * TILES + tile, g * 32 : (g + 1) * 32, :] = moved[
                    pair * 32 : (pair + 1) * 32, tile * LANES : (tile + 1) * LANES
                ]


def join_kernel(
    pieces, last_new, first_in, second_in, strips_hbm, first_hbm, second_hbm, strips, sems, out_sems
):
    stores = [
        pltpu.make_async_copy(last_new.at[0], first_hbm.at[1], out_sems.at[0]),
        pltpu.make_async_copy(last_new.at[1], second_hbm.at[1], out_sems.at[1]),
    ]
    for store in stores:
        store.start()
    perm = inverse_permutation(bf16)
    for g in range(strips.shape[0] // (8 * GROUP)):
        rows = [
            jnp.concatenate(
                [pieces[pair * TILES + tile, g * 32 : (g + 1) * 32, :] for tile in range(TILES)],
                axis=1,
            )
            for pair in range(PAIRS)
        ]
        part = pl.ds(g * 128, 128)
        strips[g * 128 : (g + 1) * 128, :] = dot(perm, jnp.concatenate(rows, axis=0)).astype(bf16)
        stores.append(pltpu.make_async_copy(strips.at[part], strips_hbm.at[part], sems.at[g]))
        stores[-1].start()
    for store in stores:
        store.wait()


def onehot(slots, level):
    dims = (128, slots.shape[1])
    out = lax.broadcasted_iota(jnp.int32, dims, 0)
    src = lax.broadcasted_iota(jnp.int32, dims, 1)
    here = slots[...] == (2 * (out >> 1) + level).astype(f32)
    return (here & ((out & 1) == (src & 1))).astype(bf16)


def place_kernel(pieces, slots, placed):
    total = pieces[0].astype(f32)
    for k in range(1, PIECES):
        total = total + pieces[k].astype(f32)
    total = total.astype(bf16)
    for level in range(2):
        lanes = slice(level * LANES, (level + 1) * LANES)
        placed[:, lanes] = dot(onehot(slots, level), total).astype(bf16)


def spread_kernel(moved, copies):
    for k in range(PIECES):
        for level in range(2):
            copies[k, level * 128 : (level + 1) * 128, :] = moved[
                :, level * LANES : (level + 1) * LANES
            ]


def step_kernel(
    gathered, left, right, first_old, second_old, piece, first_new, second_new, last_new,
    first_held, second_held, new, rows, sems, out_sems,
):
    loads = []
    for level in range(2):
        for k, (old, held) in enumerate([(first_old, first_held), (second_old, second_held)]):
            loads.append(pltpu.make_async_copy(old.at[level], held.at[level], sems.at[level, k]))
            loads[-1].start()
    replica = lax.axis_index("replica")
    pair, tile = lax.shift_right_logical(replica, 2), replica & 3
    perm = permutation(bf16)
    for level in range(2):
        parts = [
            dot(perm, left[level, g * 128 : (g + 1) * 128, :].astype(bf16)) for g in range(PAIRS)
        ]
        turned = []
        for k in range(PAIRS):
            here = jnp.concatenate([part[k * 32 : (k + 1) * 32] for part in parts], axis=0)
            rows[level, k * 128 : (k + 1) * 128, :] = here.astype(bf16)
            turned.append(here.T.astype(bf16))
        left_t = jnp.concatenate(turned, axis=1)
        right_b = right[level].astype(bf16)
        grad = jnp.concatenate(
            [
                jnp.concatenate(
                    [
                        gathered[k * TILES + t, level * 128 : (level + 1) * 128, :]
                        for t in range(TILES)
                    ],
                    axis=1,
                )
                for k in range(PAIRS)
            ],
            axis=0,
        )
        rotated = dot(dot(left_t, grad).astype(bf16), right_b)
        loads[2 * level].wait()
        loads[2 * level + 1].wait()
        first = beta_first * first_held[level].astype(f32) + (1.0 - beta_first) * rotated
        second = beta_second * second_held[level].astype(f32) + (
            (1.0 - beta_second) * rotated
        ) * rotated
        held = last_new if level else new
        held[0, :, :] = first.astype(bf16)
        held[1, :, :] = second.astype(bf16)
        if level == 0:
            stores = [
                pltpu.make_async_copy(new.at[k], out.at[0], out_sems.at[k])
                for k, out in enumerate([first_new, second_new])
            ]
            for store in stores:
                store.start()
        scaled = second * (1.0 / bias_second)
        update = (first * (1.0 / bias_first)) / (scaled * lax.rsqrt(scaled) + epsilon)
        mine = rows[level, pl.ds(pl.multiple_of(pair * 128, 128), 128), :]
        left_half = dot(mine, update.astype(bf16)).astype(bf16)
        back = right[level, pl.ds(pl.multiple_of(tile * LANES, LANES), LANES), :].astype(bf16)
        piece[:, level * LANES : (level + 1) * LANES] = lax.dot_general(
            left_half, back, (((1,), (1,)), ((), ())), preferred_element_type=f32
        ).astype(bf16)
    for store in stores:
        store.wait()


def pick_kernel(returned, slots, copies):
    mine = sum(
        lax.dot_general(
            onehot(slots, level),
            returned[:, level * LANES : (level + 1) * LANES],
            (((0,), (0,)), ((), ())),
            preferred_element_type=f32,
        )
        for level in range(2)
    ).astype(bf16)
    for k in range(PIECES):
        copies[k, :, :] = mine


VMEM = pl.BlockSpec(memory_space=pltpu.VMEM)
HBM = pl.BlockSpec(memory_space=pltpu.HBM)


def shape(dims, dtype):
    return jax.ShapeDtypeStruct(dims, dtype)


def in_hbm(array):
    return pltpu.with_memory_space_constraint(array, pltpu.HBM)


def call(kernel, out, inputs, specs=None, outs=None, scratch=(), limit=8, alias=None):
    single = not isinstance(out, (list, tuple))
    return pl.pallas_call(
        kernel,
        out_shape=out,
        in_specs=specs or [VMEM] * len(inputs),
        out_specs=outs or (VMEM if single else [VMEM] * len(out)),
        scratch_shapes=scratch,
        input_output_aliases=alias or {},
        compiler_params=pltpu.CompilerParams(vmem_limit_bytes=limit * 2**20),
    )(*inputs)


def local(grad_parts, block_owner, left_basis, right_basis, first_moment, second_moment):
    count, rows, width = grad_parts.shape[1:]
    strips = grad_parts.reshape(count * rows, width)
    slot_row = shape((1, 2 * count), f32)
    groups = count // GROUP
    pieces, slots = call(
        cut_kernel,
        [shape((PIECES, count * 2, LANES), bf16), slot_row],
        (in_hbm(block_owner[None, :]), in_hbm(strips)),
        specs=[HBM, HBM],
        scratch=[
            pltpu.VMEM((1, count), jnp.int32),
            pltpu.VMEM((count * rows, width), bf16),
            pltpu.SemaphoreType.DMA((2,)),
        ],
    )
    parts = lax.all_to_all(pieces, "replica", 0, 0)
    held = pltpu.VMEM((2, width, width), bf16)
    placed = call(place_kernel, shape((128, 2 * LANES), bf16), (parts, slots))
    moved = lax.all_to_all(placed.reshape(64, 2, 2 * LANES), "owner", 0, 0).reshape(128, 2 * LANES)
    copies = call(spread_kernel, shape((PIECES, 2 * 128, LANES), bf16), (moved,))
    gathered = lax.all_to_all(copies, "replica", 0, 0)
    in_place = pltpu.HBM((2, width, width), bf16)
    piece, first, second, last_new = call(
        step_kernel,
        [shape((128, 2 * LANES), bf16), in_place, in_place, held],
        (gathered, left_basis, right_basis, in_hbm(first_moment), in_hbm(second_moment)),
        specs=[VMEM] * 3 + [HBM] * 2,
        outs=[VMEM, HBM, HBM, VMEM],
        scratch=[held] * 4 + [pltpu.SemaphoreType.DMA((2, 2)), pltpu.SemaphoreType.DMA((2,))],
        limit=16,
    )
    returned = lax.all_to_all(piece.reshape(64, 2, 2 * LANES), "owner", 0, 0)
    copies = call(
        pick_kernel,
        shape((PIECES, count * 2, LANES), bf16),
        (returned.reshape(128, 2 * LANES), slots),
    )
    joined = lax.all_to_all(copies, "replica", 0, 0)
    direction, first, second = call(
        join_kernel,
        [
            pltpu.HBM((count * rows, width), bf16),
            in_place,
            in_place,
        ],
        (joined, last_new, in_hbm(first), in_hbm(second)),
        specs=[VMEM, VMEM, HBM, HBM],
        outs=[HBM] * 3,
        alias={2: 1, 3: 2},
        scratch=[
            pltpu.VMEM((count * rows, width), bf16),
            pltpu.SemaphoreType.DMA((groups,)),
            pltpu.SemaphoreType.DMA((2,)),
        ],
    )
    return direction.reshape(count, rows, width), first, second


def solution(mesh):
    return jax.shard_map(
        local,
        mesh=mesh,
        in_specs=(
            P("replica", None, "owner", None),
            P(),
            P("owner", None, None),
            P("owner", None, None),
            P("owner", None, None),
            P("owner", None, None),
        ),
        out_specs=(P(None, "owner", None), P("owner", None, None), P("owner", None, None)),
        check_vma=False,
    )
```

```python
import functools

import jax
import jax.numpy as jnp
from jax import lax
from jax.experimental import pallas as pl
from jax.experimental.pallas import tpu as pltpu
from jax.sharding import PartitionSpec as P

beta_first = 0.9
beta_second = 0.95
bias_first = 1.0 - 0.9**20
bias_second = 1.0 - 0.95**20
epsilon = 1e-08

PAIRS = 4
TILES = 4
PIECES = PAIRS * TILES
LANES = 128
GROUP = 16

f32 = jnp.float32
bf16 = jnp.bfloat16


def dot(a, b):
    return jnp.dot(a, b, preferred_element_type=f32)


def split(a):
    high = a.astype(bf16)
    return high, (a - high.astype(f32)).astype(bf16)


def permutation(dtype):
    out = lax.broadcasted_iota(jnp.int32, (8 * GROUP, 8 * GROUP), 0)
    src = lax.broadcasted_iota(jnp.int32, (8 * GROUP, 8 * GROUP), 1)
    pair = out >> 5
    block = (out & 31) >> 1
    return (src == block * 8 + pair * 2 + (out & 1)).astype(dtype)


def inverse_permutation(dtype):
    out = lax.broadcasted_iota(jnp.int32, (8 * GROUP, 8 * GROUP), 0)
    src = lax.broadcasted_iota(jnp.int32, (8 * GROUP, 8 * GROUP), 1)
    pair = src >> 5
    block = (src & 31) >> 1
    return (out == block * 8 + pair * 2 + (src & 1)).astype(dtype)


def cut_kernel(owner_hbm, strips_hbm, pieces, slots, owner, strips, sems):
    take = pltpu.make_async_copy(owner_hbm, owner, sems.at[0])
    take.start()
    load = pltpu.make_async_copy(strips_hbm, strips, sems.at[1])
    load.start()
    take.wait()
    count = owner.shape[1]
    across = jnp.broadcast_to(owner[...], (count, count)).astype(f32)
    earlier = lax.broadcasted_iota(jnp.int32, (count, count), 0) < lax.broadcasted_iota(
        jnp.int32, (count, count), 1
    )
    level = jnp.sum(((across == across.T) & earlier).astype(f32), axis=0, keepdims=True)
    slot = 2.0 * owner[...].astype(f32) + level
    double = lax.broadcasted_iota(jnp.int32, (count, 2 * count), 0) == (
        lax.broadcasted_iota(jnp.int32, (count, 2 * count), 1) >> 1
    )
    slots[...] = dot(slot.astype(bf16), double.astype(bf16))
    perm = permutation(bf16)
    load.wait()
    for g in range(strips.shape[0] // (8 * GROUP)):
        moved = dot(perm, strips[g * 128 : (g + 1) * 128, :]).astype(bf16)
        for pair in range(PAIRS):
            for tile in range(TILES):
                pieces[pair * TILES + tile, g * 32 : (g + 1) * 32, :] = moved[
                    pair * 32 : (pair + 1) * 32, tile * LANES : (tile + 1) * LANES
                ]


def join_kernel(
    pieces, last_new, first_in, second_in, strips_hbm, first_hbm, second_hbm, strips, sems, out_sems
):
    stores = [
        pltpu.make_async_copy(last_new.at[0], first_hbm.at[1], out_sems.at[0]),
        pltpu.make_async_copy(last_new.at[1], second_hbm.at[1], out_sems.at[1]),
    ]
    for store in stores:
        store.start()
    perm = inverse_permutation(bf16)
    for g in range(strips.shape[0] // (8 * GROUP)):
        rows = [
            jnp.concatenate(
                [pieces[pair * TILES + tile, g * 32 : (g + 1) * 32, :] for tile in range(TILES)],
                axis=1,
            )
            for pair in range(PAIRS)
        ]
        part = pl.ds(g * 128, 128)
        strips[g * 128 : (g + 1) * 128, :] = dot(perm, jnp.concatenate(rows, axis=0)).astype(bf16)
        stores.append(pltpu.make_async_copy(strips.at[part], strips_hbm.at[part], sems.at[g]))
        stores[-1].start()
    for store in stores:
        store.wait()


def onehot(slots, level):
    dims = (128, slots.shape[1])
    out = lax.broadcasted_iota(jnp.int32, dims, 0)
    src = lax.broadcasted_iota(jnp.int32, dims, 1)
    here = slots[...] == (2 * (out >> 1) + level).astype(f32)
    return (here & ((out & 1) == (src & 1))).astype(bf16)


def place_kernel(pieces, slots, placed):
    total = pieces[0].astype(f32)
    for k in range(1, PIECES):
        total = total + pieces[k].astype(f32)
    total = total.astype(bf16)
    for level in range(2):
        lanes = slice(level * LANES, (level + 1) * LANES)
        placed[:, lanes] = dot(onehot(slots, level), total).astype(bf16)


def spread_kernel(moved, copies):
    for k in range(PIECES):
        for level in range(2):
            copies[k, level * 128 : (level + 1) * 128, :] = moved[
                :, level * LANES : (level + 1) * LANES
            ]


def step_kernel(
    gathered, left, right, first_old, second_old, piece, first_new, second_new, last_new,
    second_held, new, rows, sems, out_sems,
):
    loads = []
    for level in range(2):
        for k, (old, held) in enumerate([(second_old, second_held)]):
            loads.append(pltpu.make_async_copy(old.at[level], held.at[level], sems.at[level, k]))
            loads[-1].start()
    replica = lax.axis_index("replica")
    pair, tile = lax.shift_right_logical(replica, 2), replica & 3
    perm = permutation(bf16)
    perm2 = jnp.concatenate([perm, perm], axis=1)
    for level in range(2):
        parts = [
            dot(perm2, jnp.concatenate(split(left[level, g * 128 : (g + 1) * 128, :]), axis=0))
            for g in range(PAIRS)
        ]
        turned = []
        for k in range(PAIRS):
            here = jnp.concatenate([part[k * 32 : (k + 1) * 32] for part in parts], axis=0)
            rows[level, k * 128 : (k + 1) * 128, :] = here.astype(bf16)
            turned.append(here.T)
        left_high, left_low = split(jnp.concatenate(turned, axis=1))
        right_high, right_low = split(right[level])
        grad = jnp.concatenate(
            [
                jnp.concatenate(
                    [
                        gathered[k * TILES + t, level * 128 : (level + 1) * 128, :]
                        for t in range(TILES)
                    ],
                    axis=1,
                )
                for k in range(PAIRS)
            ],
            axis=0,
        )
        half_high, half_low = split(dot(left_high, grad) + dot(left_low, grad))
        rotated = dot(half_high, right_high) + (
            dot(half_high, right_low) + dot(half_low, right_high)
        )
        loads[level].wait()
        first = beta_first * first_old[level].astype(f32) + (1.0 - beta_first) * rotated
        second = beta_second * second_held[level].astype(f32) + (
            (1.0 - beta_second) * rotated
        ) * rotated
        held = last_new if level else new
        held[0, :, :] = first.astype(bf16)
        held[1, :, :] = second.astype(bf16)
        if level == 0:
            stores = [
                pltpu.make_async_copy(new.at[k], out.at[0], out_sems.at[k])
                for k, out in enumerate([first_new, second_new])
            ]
            for store in stores:
                store.start()
        scaled = second * (1.0 / bias_second)
        update = (first * (1.0 / bias_first)) / (scaled * lax.rsqrt(scaled) + epsilon)
        mine = rows[level, pl.ds(pl.multiple_of(pair * 128, 128), 128), :]
        left_half = dot(mine, update.astype(bf16)).astype(bf16)
        back = right[level, pl.ds(pl.multiple_of(tile * LANES, LANES), LANES), :].astype(bf16)
        piece[:, level * LANES : (level + 1) * LANES] = lax.dot_general(
            left_half, back, (((1,), (1,)), ((), ())), preferred_element_type=f32
        ).astype(bf16)
    for store in stores:
        store.wait()


def pick_kernel(returned, slots, copies):
    mine = sum(
        lax.dot_general(
            onehot(slots, level),
            returned[:, level * LANES : (level + 1) * LANES],
            (((0,), (0,)), ((), ())),
            preferred_element_type=f32,
        )
        for level in range(2)
    ).astype(bf16)
    for k in range(PIECES):
        copies[k, :, :] = mine


VMEM = pl.BlockSpec(memory_space=pltpu.VMEM)
HBM = pl.BlockSpec(memory_space=pltpu.HBM)


def shape(dims, dtype):
    return jax.ShapeDtypeStruct(dims, dtype)


def in_hbm(array):
    return pltpu.with_memory_space_constraint(array, pltpu.HBM)


def call(kernel, out, inputs, specs=None, outs=None, scratch=(), limit=8, alias=None):
    single = not isinstance(out, (list, tuple))
    return pl.pallas_call(
        kernel,
        out_shape=out,
        in_specs=specs or [VMEM] * len(inputs),
        out_specs=outs or (VMEM if single else [VMEM] * len(out)),
        scratch_shapes=scratch,
        input_output_aliases=alias or {},
        compiler_params=pltpu.CompilerParams(vmem_limit_bytes=limit * 2**20),
    )(*inputs)


def local(grad_parts, block_owner, left_basis, right_basis, first_moment, second_moment):
    count, rows, width = grad_parts.shape[1:]
    strips = grad_parts.reshape(count * rows, width)
    slot_row = shape((1, 2 * count), f32)
    groups = count // GROUP
    pieces, slots = call(
        cut_kernel,
        [shape((PIECES, count * 2, LANES), bf16), slot_row],
        (in_hbm(block_owner[None, :]), in_hbm(strips)),
        specs=[HBM, HBM],
        scratch=[
            pltpu.VMEM((1, count), jnp.int32),
            pltpu.VMEM((count * rows, width), bf16),
            pltpu.SemaphoreType.DMA((2,)),
        ],
    )
    parts = lax.all_to_all(pieces, "replica", 0, 0)
    held = pltpu.VMEM((2, width, width), bf16)
    placed = call(place_kernel, shape((128, 2 * LANES), bf16), (parts, slots))
    moved = lax.all_to_all(placed.reshape(64, 2, 2 * LANES), "owner", 0, 0).reshape(128, 2 * LANES)
    copies = call(spread_kernel, shape((PIECES, 2 * 128, LANES), bf16), (moved,))
    gathered = lax.all_to_all(copies, "replica", 0, 0)
    in_place = pltpu.HBM((2, width, width), bf16)
    piece, first, second, last_new = call(
        step_kernel,
        [shape((128, 2 * LANES), bf16), in_place, in_place, held],
        (gathered, left_basis, right_basis, first_moment, in_hbm(second_moment)),
        specs=[VMEM] * 4 + [HBM],
        outs=[VMEM, HBM, HBM, VMEM],
        scratch=[held] * 3 + [pltpu.SemaphoreType.DMA((2, 1)), pltpu.SemaphoreType.DMA((2,))],
        limit=16,
    )
    returned = lax.all_to_all(piece.reshape(64, 2, 2 * LANES), "owner", 0, 0)
    copies = call(
        pick_kernel,
        shape((PIECES, count * 2, LANES), bf16),
        (returned.reshape(128, 2 * LANES), slots),
    )
    joined = lax.all_to_all(copies, "replica", 0, 0)
    direction, first, second = call(
        join_kernel,
        [
            pltpu.HBM((count * rows, width), bf16),
            in_place,
            in_place,
        ],
        (joined, last_new, in_hbm(first), in_hbm(second)),
        specs=[VMEM, VMEM, HBM, HBM],
        outs=[HBM] * 3,
        alias={2: 1, 3: 2},
        scratch=[
            pltpu.VMEM((count * rows, width), bf16),
            pltpu.SemaphoreType.DMA((groups,)),
            pltpu.SemaphoreType.DMA((2,)),
        ],
    )
    return direction.reshape(count, rows, width), first, second


def solution(mesh):
    return jax.shard_map(
        local,
        mesh=mesh,
        in_specs=(
            P("replica", None, "owner", None),
            P(),
            P("owner", None, None),
            P("owner", None, None),
            P("owner", None, None),
            P("owner", None, None),
        ),
        out_specs=(P(None, "owner", None), P("owner", None, None), P("owner", None, None)),
        check_vma=False,
    )
```

```python
import functools

import jax
import jax.numpy as jnp
from jax import lax
from jax.experimental import pallas as pl
from jax.experimental.pallas import tpu as pltpu
from jax.sharding import PartitionSpec as P

beta_first = 0.9
beta_second = 0.95
bias_first = 1.0 - 0.9**20
bias_second = 1.0 - 0.95**20
epsilon = 1e-08

PAIRS = 4
TILES = 4
PIECES = PAIRS * TILES
LANES = 128
GROUP = 16

f32 = jnp.float32
bf16 = jnp.bfloat16


def dot(a, b):
    return jnp.dot(a, b, preferred_element_type=f32)


def dot_t(a, b):
    return lax.dot_general(a, b, (((0,), (0,)), ((), ())), preferred_element_type=f32)


def split(a):
    high = a.astype(bf16)
    return high, (a - high.astype(f32)).astype(bf16)


def permutation(dtype):
    out = lax.broadcasted_iota(jnp.int32, (8 * GROUP, 8 * GROUP), 0)
    src = lax.broadcasted_iota(jnp.int32, (8 * GROUP, 8 * GROUP), 1)
    pair = out >> 5
    block = (out & 31) >> 1
    return (src == block * 8 + pair * 2 + (out & 1)).astype(dtype)


def inverse_permutation(dtype):
    out = lax.broadcasted_iota(jnp.int32, (8 * GROUP, 8 * GROUP), 0)
    src = lax.broadcasted_iota(jnp.int32, (8 * GROUP, 8 * GROUP), 1)
    pair = src >> 5
    block = (src & 31) >> 1
    return (out == block * 8 + pair * 2 + (src & 1)).astype(dtype)


def cut_kernel(owner_hbm, strips_hbm, pieces, slots, owner, strips, sems):
    take = pltpu.make_async_copy(owner_hbm, owner, sems.at[0])
    take.start()
    load = pltpu.make_async_copy(strips_hbm, strips, sems.at[1])
    load.start()
    take.wait()
    count = owner.shape[1]
    across = jnp.broadcast_to(owner[...], (count, count)).astype(f32)
    earlier = lax.broadcasted_iota(jnp.int32, (count, count), 0) < lax.broadcasted_iota(
        jnp.int32, (count, count), 1
    )
    level = jnp.sum(((across == across.T) & earlier).astype(f32), axis=0, keepdims=True)
    slot = 2.0 * owner[...].astype(f32) + level
    double = lax.broadcasted_iota(jnp.int32, (count, 2 * count), 0) == (
        lax.broadcasted_iota(jnp.int32, (count, 2 * count), 1) >> 1
    )
    slots[...] = dot(slot.astype(bf16), double.astype(bf16))
    perm = permutation(bf16)
    load.wait()
    for g in range(strips.shape[0] // (8 * GROUP)):
        moved = dot(perm, strips[g * 128 : (g + 1) * 128, :]).astype(bf16)
        for pair in range(PAIRS):
            for tile in range(TILES):
                pieces[pair * TILES + tile, g * 32 : (g + 1) * 32, :] = moved[
                    pair * 32 : (pair + 1) * 32, tile * LANES : (tile + 1) * LANES
                ]


def join_kernel(
    pieces, last_new, first_in, second_in, strips_hbm, first_hbm, second_hbm, strips, sems, out_sems
):
    stores = [
        pltpu.make_async_copy(last_new.at[0], first_hbm.at[1], out_sems.at[0]),
        pltpu.make_async_copy(last_new.at[1], second_hbm.at[1], out_sems.at[1]),
    ]
    for store in stores:
        store.start()
    perm = inverse_permutation(bf16)
    for g in range(strips.shape[0] // (8 * GROUP)):
        rows = [
            jnp.concatenate(
                [pieces[pair * TILES + tile, g * 32 : (g + 1) * 32, :] for tile in range(TILES)],
                axis=1,
            )
            for pair in range(PAIRS)
        ]
        part = pl.ds(g * 128, 128)
        strips[g * 128 : (g + 1) * 128, :] = dot(perm, jnp.concatenate(rows, axis=0)).astype(bf16)
        stores.append(pltpu.make_async_copy(strips.at[part], strips_hbm.at[part], sems.at[g]))
        stores[-1].start()
    for store in stores:
        store.wait()


def onehot(slots, level):
    dims = (128, slots.shape[1])
    out = lax.broadcasted_iota(jnp.int32, dims, 0)
    src = lax.broadcasted_iota(jnp.int32, dims, 1)
    here = slots[...] == (2 * (out >> 1) + level).astype(f32)
    return (here & ((out & 1) == (src & 1))).astype(bf16)


def place_kernel(pieces, slots, placed):
    total = pieces[0].astype(f32)
    for k in range(1, PIECES):
        total = total + pieces[k].astype(f32)
    total = total.astype(bf16)
    for level in range(2):
        lanes = slice(level * LANES, (level + 1) * LANES)
        placed[:, lanes] = dot(onehot(slots, level), total).astype(bf16)


def spread_kernel(moved, copies):
    for k in range(PIECES):
        for level in range(2):
            copies[k, level * 128 : (level + 1) * 128, :] = moved[
                :, level * LANES : (level + 1) * LANES
            ]


def step_kernel(
    gathered, left, right, first_old, second_old, piece, first_new, second_new, last_new,
    first_held, second_held, new, sems, out_sems,
):
    loads = []
    for level in range(2):
        for k, (old, held) in enumerate([(first_old, first_held), (second_old, second_held)]):
            loads.append(pltpu.make_async_copy(old.at[level], held.at[level], sems.at[level, k]))
            loads[-1].start()
    replica = lax.axis_index("replica")
    pair, tile = lax.shift_right_logical(replica, 2), replica & 3
    perm = inverse_permutation(bf16)
    out = lax.broadcasted_iota(jnp.int32, (2 * GROUP, 8 * GROUP), 0)
    src = lax.broadcasted_iota(jnp.int32, (2 * GROUP, 8 * GROUP), 1)
    mine_of = (src == (out >> 1) * 8 + pair * 2 + (out & 1)).astype(bf16)
    for level in range(2):
        grad = jnp.concatenate(
            [
                dot(
                    perm,
                    jnp.concatenate(
                        [
                            jnp.concatenate(
                                [
                                    gathered[
                                        k * TILES + t,
                                        level * 128 + g * 32 : level * 128 + (g + 1) * 32,
                                        :,
                                    ]
                                    for t in range(TILES)
                                ],
                                axis=1,
                            )
                            for k in range(PAIRS)
                        ],
                        axis=0,
                    ),
                ).astype(bf16)
                for g in range(PAIRS)
            ],
            axis=0,
        )
        left_high, left_low = split(left[level])
        right_high, right_low = split(right[level])
        half_high, half_low = split(dot_t(left_high, grad) + dot_t(left_low, grad))
        rotated = dot(half_high, right_high) + (
            dot(half_high, right_low) + dot(half_low, right_high)
        )
        loads[2 * level].wait()
        loads[2 * level + 1].wait()
        first = beta_first * first_held[level].astype(f32) + (1.0 - beta_first) * rotated
        second = beta_second * second_held[level].astype(f32) + (
            (1.0 - beta_second) * rotated
        ) * rotated
        held = last_new if level else new
        held[0, :, :] = first.astype(bf16)
        held[1, :, :] = second.astype(bf16)
        if level == 0:
            stores = [
                pltpu.make_async_copy(new.at[k], out.at[0], out_sems.at[k])
                for k, out in enumerate([first_new, second_new])
            ]
            for store in stores:
                store.start()
        scaled = second * (1.0 / bias_second)
        update = (first * (1.0 / bias_first)) / (scaled * lax.rsqrt(scaled) + epsilon)
        mine = jnp.concatenate(
            [dot(mine_of, left_high[g * 128 : (g + 1) * 128]) for g in range(PAIRS)], axis=0
        ).astype(bf16)
        left_half = dot(mine, update.astype(bf16)).astype(bf16)
        back = right[level, pl.ds(pl.multiple_of(tile * LANES, LANES), LANES), :].astype(bf16)
        piece[:, level * LANES : (level + 1) * LANES] = lax.dot_general(
            left_half, back, (((1,), (1,)), ((), ())), preferred_element_type=f32
        ).astype(bf16)
    for store in stores:
        store.wait()


def pick_kernel(returned, slots, copies):
    mine = sum(
        lax.dot_general(
            onehot(slots, level),
            returned[:, level * LANES : (level + 1) * LANES],
            (((0,), (0,)), ((), ())),
            preferred_element_type=f32,
        )
        for level in range(2)
    ).astype(bf16)
    for k in range(PIECES):
        copies[k, :, :] = mine


VMEM = pl.BlockSpec(memory_space=pltpu.VMEM)
HBM = pl.BlockSpec(memory_space=pltpu.HBM)


def shape(dims, dtype):
    return jax.ShapeDtypeStruct(dims, dtype)


def in_hbm(array):
    return pltpu.with_memory_space_constraint(array, pltpu.HBM)


def call(kernel, out, inputs, specs=None, outs=None, scratch=(), limit=8, alias=None):
    single = not isinstance(out, (list, tuple))
    return pl.pallas_call(
        kernel,
        out_shape=out,
        in_specs=specs or [VMEM] * len(inputs),
        out_specs=outs or (VMEM if single else [VMEM] * len(out)),
        scratch_shapes=scratch,
        input_output_aliases=alias or {},
        compiler_params=pltpu.CompilerParams(vmem_limit_bytes=limit * 2**20),
    )(*inputs)


def local(grad_parts, block_owner, left_basis, right_basis, first_moment, second_moment):
    count, rows, width = grad_parts.shape[1:]
    strips = grad_parts.reshape(count * rows, width)
    slot_row = shape((1, 2 * count), f32)
    groups = count // GROUP
    pieces, slots = call(
        cut_kernel,
        [shape((PIECES, count * 2, LANES), bf16), slot_row],
        (in_hbm(block_owner[None, :]), in_hbm(strips)),
        specs=[HBM, HBM],
        scratch=[
            pltpu.VMEM((1, count), jnp.int32),
            pltpu.VMEM((count * rows, width), bf16),
            pltpu.SemaphoreType.DMA((2,)),
        ],
    )
    parts = lax.all_to_all(pieces, "replica", 0, 0)
    held = pltpu.VMEM((2, width, width), bf16)
    placed = call(place_kernel, shape((128, 2 * LANES), bf16), (parts, slots))
    moved = lax.all_to_all(placed.reshape(64, 2, 2 * LANES), "owner", 0, 0).reshape(128, 2 * LANES)
    copies = call(spread_kernel, shape((PIECES, 2 * 128, LANES), bf16), (moved,))
    gathered = lax.all_to_all(copies, "replica", 0, 0)
    in_place = pltpu.HBM((2, width, width), bf16)
    piece, first, second, last_new = call(
        step_kernel,
        [shape((128, 2 * LANES), bf16), in_place, in_place, held],
        (gathered, left_basis, right_basis, in_hbm(first_moment), in_hbm(second_moment)),
        specs=[VMEM] * 3 + [HBM] * 2,
        outs=[VMEM, HBM, HBM, VMEM],
        scratch=[held] * 3 + [pltpu.SemaphoreType.DMA((2, 2)), pltpu.SemaphoreType.DMA((2,))],
        limit=16,
    )
    returned = lax.all_to_all(piece.reshape(64, 2, 2 * LANES), "owner", 0, 0)
    copies = call(
        pick_kernel,
        shape((PIECES, count * 2, LANES), bf16),
        (returned.reshape(128, 2 * LANES), slots),
    )
    joined = lax.all_to_all(copies, "replica", 0, 0)
    direction, first, second = call(
        join_kernel,
        [
            pltpu.HBM((count * rows, width), bf16),
            in_place,
            in_place,
        ],
        (joined, last_new, in_hbm(first), in_hbm(second)),
        specs=[VMEM, VMEM, HBM, HBM],
        outs=[HBM] * 3,
        alias={2: 1, 3: 2},
        scratch=[
            pltpu.VMEM((count * rows, width), bf16),
            pltpu.SemaphoreType.DMA((groups,)),
            pltpu.SemaphoreType.DMA((2,)),
        ],
    )
    return direction.reshape(count, rows, width), first, second


def solution(mesh):
    return jax.shard_map(
        local,
        mesh=mesh,
        in_specs=(
            P("replica", None, "owner", None),
            P(),
            P("owner", None, None),
            P("owner", None, None),
            P("owner", None, None),
            P("owner", None, None),
        ),
        out_specs=(P(None, "owner", None), P("owner", None, None), P("owner", None, None)),
        check_vma=False,
    )
```

```python
import functools

import jax
import jax.numpy as jnp
from jax import lax
from jax.experimental import pallas as pl
from jax.experimental.pallas import tpu as pltpu
from jax.sharding import PartitionSpec as P

beta_first = 0.9
beta_second = 0.95
bias_first = 1.0 - 0.9**20
bias_second = 1.0 - 0.95**20
epsilon = 1e-08

PAIRS = 4
TILES = 4
PIECES = PAIRS * TILES
LANES = 128
GROUP = 16

f32 = jnp.float32
bf16 = jnp.bfloat16


def dot(a, b):
    return jnp.dot(a, b, preferred_element_type=f32)


def dot_t(a, b):
    return lax.dot_general(a, b, (((0,), (0,)), ((), ())), preferred_element_type=f32)


def split(a):
    high = a.astype(bf16)
    return high, (a - high.astype(f32)).astype(bf16)


def permutation(dtype):
    out = lax.broadcasted_iota(jnp.int32, (8 * GROUP, 8 * GROUP), 0)
    src = lax.broadcasted_iota(jnp.int32, (8 * GROUP, 8 * GROUP), 1)
    pair = out >> 5
    block = (out & 31) >> 1
    return (src == block * 8 + pair * 2 + (out & 1)).astype(dtype)


def inverse_permutation(dtype):
    out = lax.broadcasted_iota(jnp.int32, (8 * GROUP, 8 * GROUP), 0)
    src = lax.broadcasted_iota(jnp.int32, (8 * GROUP, 8 * GROUP), 1)
    pair = src >> 5
    block = (src & 31) >> 1
    return (out == block * 8 + pair * 2 + (src & 1)).astype(dtype)


def cut_kernel(owner_hbm, strips_hbm, pieces, slots, owner, strips, sems):
    take = pltpu.make_async_copy(owner_hbm, owner, sems.at[0])
    take.start()
    load = pltpu.make_async_copy(strips_hbm, strips, sems.at[1])
    load.start()
    take.wait()
    count = owner.shape[1]
    across = jnp.broadcast_to(owner[...], (count, count)).astype(f32)
    earlier = lax.broadcasted_iota(jnp.int32, (count, count), 0) < lax.broadcasted_iota(
        jnp.int32, (count, count), 1
    )
    level = jnp.sum(((across == across.T) & earlier).astype(f32), axis=0, keepdims=True)
    slot = 2.0 * owner[...].astype(f32) + level
    double = lax.broadcasted_iota(jnp.int32, (count, 2 * count), 0) == (
        lax.broadcasted_iota(jnp.int32, (count, 2 * count), 1) >> 1
    )
    slots[...] = dot(slot.astype(bf16), double.astype(bf16))
    perm = permutation(bf16)
    load.wait()
    for g in range(strips.shape[0] // (8 * GROUP)):
        moved = dot(perm, strips[g * 128 : (g + 1) * 128, :]).astype(bf16)
        for pair in range(PAIRS):
            for tile in range(TILES):
                pieces[pair * TILES + tile, g * 32 : (g + 1) * 32, :] = moved[
                    pair * 32 : (pair + 1) * 32, tile * LANES : (tile + 1) * LANES
                ]


def join_kernel(
    pieces, last_new, first_in, second_in, strips_hbm, first_hbm, second_hbm, strips, sems, out_sems
):
    stores = [
        pltpu.make_async_copy(last_new.at[0], first_hbm.at[1], out_sems.at[0]),
        pltpu.make_async_copy(last_new.at[1], second_hbm.at[1], out_sems.at[1]),
    ]
    for store in stores:
        store.start()
    perm = inverse_permutation(bf16)
    for g in range(strips.shape[0] // (8 * GROUP)):
        rows = [
            jnp.concatenate(
                [pieces[pair * TILES + tile, g * 32 : (g + 1) * 32, :] for tile in range(TILES)],
                axis=1,
            )
            for pair in range(PAIRS)
        ]
        part = pl.ds(g * 128, 128)
        strips[g * 128 : (g + 1) * 128, :] = dot(perm, jnp.concatenate(rows, axis=0)).astype(bf16)
        stores.append(pltpu.make_async_copy(strips.at[part], strips_hbm.at[part], sems.at[g]))
        stores[-1].start()
    for store in stores:
        store.wait()


def onehot(slots, level):
    dims = (128, slots.shape[1])
    out = lax.broadcasted_iota(jnp.int32, dims, 0)
    src = lax.broadcasted_iota(jnp.int32, dims, 1)
    here = slots[...] == (2 * (out >> 1) + level).astype(f32)
    return (here & ((out & 1) == (src & 1))).astype(bf16)


def place_kernel(pieces, slots, placed):
    total = pieces[0].astype(f32)
    for k in range(1, PIECES):
        total = total + pieces[k].astype(f32)
    total = total.astype(bf16)
    for level in range(2):
        lanes = slice(level * LANES, (level + 1) * LANES)
        placed[:, lanes] = dot(onehot(slots, level), total).astype(bf16)


def spread_kernel(moved, copies):
    for k in range(PIECES):
        for level in range(2):
            copies[k, level * 128 : (level + 1) * 128, :] = moved[
                :, level * LANES : (level + 1) * LANES
            ]


def step_kernel(
    gathered, left, right, first_old, second_old, piece, first_new, second_new, last_new,
    first_held, second_held, new, sems, out_sems,
):
    loads = []
    for level in range(2):
        for k, (old, held) in enumerate([(first_old, first_held), (second_old, second_held)]):
            loads.append(pltpu.make_async_copy(old.at[level], held.at[level], sems.at[level, k]))
            loads[-1].start()
    replica = lax.axis_index("replica")
    pair, tile = lax.shift_right_logical(replica, 2), replica & 3
    perm = inverse_permutation(bf16)
    out = lax.broadcasted_iota(jnp.int32, (2 * GROUP, 8 * GROUP), 0)
    src = lax.broadcasted_iota(jnp.int32, (2 * GROUP, 8 * GROUP), 1)
    mine_of = (src == (out >> 1) * 8 + pair * 2 + (out & 1)).astype(bf16)
    for level in range(2):
        grad = jnp.concatenate(
            [
                dot(
                    perm,
                    jnp.concatenate(
                        [
                            jnp.concatenate(
                                [
                                    gathered[
                                        k * TILES + t,
                                        level * 128 + g * 32 : level * 128 + (g + 1) * 32,
                                        :,
                                    ]
                                    for t in range(TILES)
                                ],
                                axis=1,
                            )
                            for k in range(PAIRS)
                        ],
                        axis=0,
                    ),
                ).astype(bf16)
                for g in range(PAIRS)
            ],
            axis=0,
        )
        left_high, left_low = split(left[level])
        right_high, right_low = split(right[level])
        half_high, half_low = split(dot_t(left_high, grad) + dot_t(left_low, grad))
        rotated = dot(half_high, right_high) + (
            dot(half_high, right_low) + dot(half_low, right_high)
        )
        loads[2 * level].wait()
        loads[2 * level + 1].wait()
        first = beta_first * first_held[level].astype(f32) + (1.0 - beta_first) * rotated
        second = beta_second * second_held[level].astype(f32) + (
            (1.0 - beta_second) * rotated
        ) * rotated
        held = last_new if level else new
        held[0, :, :] = first.astype(bf16)
        held[1, :, :] = second.astype(bf16)
        if level == 0:
            stores = [
                pltpu.make_async_copy(new.at[k], out.at[0], out_sems.at[k])
                for k, out in enumerate([first_new, second_new])
            ]
            for store in stores:
                store.start()
        root = second * lax.rsqrt(second)
        update = first / (root * (bias_first / bias_second**0.5) + bias_first * epsilon)
        mine = jnp.concatenate(
            [dot(mine_of, left_high[g * 128 : (g + 1) * 128]) for g in range(PAIRS)], axis=0
        ).astype(bf16)
        left_half = dot(mine, update.astype(bf16)).astype(bf16)
        back = right[level, pl.ds(pl.multiple_of(tile * LANES, LANES), LANES), :].astype(bf16)
        piece[:, level * LANES : (level + 1) * LANES] = lax.dot_general(
            left_half, back, (((1,), (1,)), ((), ())), preferred_element_type=f32
        ).astype(bf16)
    for store in stores:
        store.wait()


def pick_kernel(returned, slots, copies):
    mine = sum(
        lax.dot_general(
            onehot(slots, level),
            returned[:, level * LANES : (level + 1) * LANES],
            (((0,), (0,)), ((), ())),
            preferred_element_type=f32,
        )
        for level in range(2)
    ).astype(bf16)
    for k in range(PIECES):
        copies[k, :, :] = mine


VMEM = pl.BlockSpec(memory_space=pltpu.VMEM)
HBM = pl.BlockSpec(memory_space=pltpu.HBM)


def shape(dims, dtype):
    return jax.ShapeDtypeStruct(dims, dtype)


def in_hbm(array):
    return pltpu.with_memory_space_constraint(array, pltpu.HBM)


def call(kernel, out, inputs, specs=None, outs=None, scratch=(), limit=8, alias=None):
    single = not isinstance(out, (list, tuple))
    return pl.pallas_call(
        kernel,
        out_shape=out,
        in_specs=specs or [VMEM] * len(inputs),
        out_specs=outs or (VMEM if single else [VMEM] * len(out)),
        scratch_shapes=scratch,
        input_output_aliases=alias or {},
        compiler_params=pltpu.CompilerParams(vmem_limit_bytes=limit * 2**20),
    )(*inputs)


def local(grad_parts, block_owner, left_basis, right_basis, first_moment, second_moment):
    count, rows, width = grad_parts.shape[1:]
    strips = grad_parts.reshape(count * rows, width)
    slot_row = shape((1, 2 * count), f32)
    groups = count // GROUP
    pieces, slots = call(
        cut_kernel,
        [shape((PIECES, count * 2, LANES), bf16), slot_row],
        (in_hbm(block_owner[None, :]), in_hbm(strips)),
        specs=[HBM, HBM],
        scratch=[
            pltpu.VMEM((1, count), jnp.int32),
            pltpu.VMEM((count * rows, width), bf16),
            pltpu.SemaphoreType.DMA((2,)),
        ],
    )
    parts = lax.all_to_all(pieces, "replica", 0, 0)
    held = pltpu.VMEM((2, width, width), bf16)
    placed = call(place_kernel, shape((128, 2 * LANES), bf16), (parts, slots))
    moved = lax.all_to_all(placed.reshape(64, 2, 2 * LANES), "owner", 0, 0).reshape(128, 2 * LANES)
    copies = call(spread_kernel, shape((PIECES, 2 * 128, LANES), bf16), (moved,))
    gathered = lax.all_to_all(copies, "replica", 0, 0)
    in_place = pltpu.HBM((2, width, width), bf16)
    piece, first, second, last_new = call(
        step_kernel,
        [shape((128, 2 * LANES), bf16), in_place, in_place, held],
        (gathered, left_basis, right_basis, in_hbm(first_moment), in_hbm(second_moment)),
        specs=[VMEM] * 3 + [HBM] * 2,
        outs=[VMEM, HBM, HBM, VMEM],
        scratch=[held] * 3 + [pltpu.SemaphoreType.DMA((2, 2)), pltpu.SemaphoreType.DMA((2,))],
        limit=16,
    )
    returned = lax.all_to_all(piece.reshape(64, 2, 2 * LANES), "owner", 0, 0)
    copies = call(
        pick_kernel,
        shape((PIECES, count * 2, LANES), bf16),
        (returned.reshape(128, 2 * LANES), slots),
    )
    joined = lax.all_to_all(copies, "replica", 0, 0)
    direction, first, second = call(
        join_kernel,
        [
            pltpu.HBM((count * rows, width), bf16),
            in_place,
            in_place,
        ],
        (joined, last_new, in_hbm(first), in_hbm(second)),
        specs=[VMEM, VMEM, HBM, HBM],
        outs=[HBM] * 3,
        alias={2: 1, 3: 2},
        scratch=[
            pltpu.VMEM((count * rows, width), bf16),
            pltpu.SemaphoreType.DMA((groups,)),
            pltpu.SemaphoreType.DMA((2,)),
        ],
    )
    return direction.reshape(count, rows, width), first, second


def solution(mesh):
    return jax.shard_map(
        local,
        mesh=mesh,
        in_specs=(
            P("replica", None, "owner", None),
            P(),
            P("owner", None, None),
            P("owner", None, None),
            P("owner", None, None),
            P("owner", None, None),
        ),
        out_specs=(P(None, "owner", None), P("owner", None, None), P("owner", None, None)),
        check_vma=False,
    )
```
